256 devices in a mesh: inst: 64 (over z, y_lo, x), space: 4 (over y_hi, core).
Axes of the slice: x: 4, y: 4 (y_hi: 2, y_lo: 2; y = y_hi * 2 + y_lo), z: 8, core: 2. Of those that a mesh axis runs over, the one named last changes fastest.
Arguments:
- base_state: float32 [256, 5, 64, 512], P('inst', None, 'space'), may hold values from -3 to 3
- adjoint: float32 [256, 5, 64, 512], P('inst', None, 'space'), may hold values from -6 to 6
- gradient: float32 [256, 5, 64, 512], P('inst', None, 'space'), may hold values from -6 to 6
- cell_types: int32 [64, 512], P('space'), may hold values from 0 to 2
Outputs:
- adjoint_residual: float32 [256, 5, 64, 512], P('inst', None, 'space')
The draws below stay inside these ranges and needn't reach their ends.
Inputs may be any that keep to these rules, and one draw needn't show every extreme that they name: `cell_types`: 0 marks plasma cells, 1 wall cells, 2 anode injection cells.
All inputs are finite; a program needn't handle non-finite values.
Results may differ from the reference program's by a relative error of at most 0.00005.
Values sent between devices are 32-bit elements; how exact they have to be, the bound alone decides.
No kernel may reach another device: no remote copies, remote signals or barrier semaphores. Data moves between devices by JAX's collectives and lax.ppermute only.
A program may use at most 64 MiB of HBM per device.

```python
import jax
import jax.numpy as jnp
from jax import lax

FIELDS = 5
RAD = 512
INSTANCES = 256
AXIAL = 64


def place_ends(entries, stream_key, smallest, largest):
    extent = entries.shape
    index_at = [jax.random.randint(jax.random.fold_in(stream_key, axis), (), 0, extent[axis]) for axis in range(len(extent))]
    entries = entries.at[tuple(index_at)].set(smallest)
    longest = extent.index(max(extent))
    index_at[longest] = (index_at[longest] + 1) % extent[longest]
    return entries.at[tuple(index_at)].set(largest)


def levels(rng, extent, cuts, least, top_value):
    loudness, own = 1.0, jax.random.fold_in(rng, 6)
    for dim, shards_of in cuts:
        steps = jnp.exp(jax.random.uniform(jax.random.fold_in(own, dim), (shards_of,), jnp.float32, least / len(cuts), top_value / len(cuts)))
        loudness = loudness * jnp.repeat(steps, extent[dim] // shards_of).reshape([-1 if axis == dim else 1 for axis in range(len(extent))])
    return loudness


def gaussian(own_key, extent, scale, limit, pieces=(), dtype=jnp.bfloat16):
    result = scale * jax.random.normal(own_key, extent, jnp.float32)
    if pieces:
        result = result * levels(own_key, extent, pieces, -0.22, 0.18)
    return jnp.clip(result, -limit, limit).astype(dtype)


def setup_inputs(seed: int = 0) -> dict:
    splits = jax.random.split(jax.random.key(seed), 5)
    base_state = gaussian(splits[0], (INSTANCES, FIELDS, AXIAL, RAD), 0.5, 3.0, ((0, 64), (2, 4)), jnp.float32)
    adjoint = gaussian(splits[1], (INSTANCES, FIELDS, AXIAL, RAD), 1.0, 6.0, ((0, 64), (2, 4)), jnp.float32)
    gradient = gaussian(splits[2], (INSTANCES, FIELDS, AXIAL, RAD), 1.0, 6.0, ((0, 64), (2, 4)), jnp.float32)
    cell_types = place_ends(jax.random.randint(splits[3], (AXIAL, RAD), 0, 3), jax.random.fold_in(splits[3], 1), 0, 2).astype(jnp.int32)
    return dict(base_state=base_state, adjoint=adjoint, gradient=gradient, cell_types=cell_types)


dissipation = 0.5
ionize_rate = 0.6
collide_rate = 0.4
energy_loss = 0.3
field_push = 0.8
wall_relax = 2.0
time_factor = 4.0

def axial_flux(state):
    ion_log, axial_vel, radial_vel, neutral_log, temper = (state[0], state[1], state[2], state[3], state[4])
    return jnp.stack([jnp.exp(ion_log) * axial_vel, 0.5 * axial_vel * axial_vel + temper, axial_vel * radial_vel, jnp.exp(neutral_log), axial_vel * temper], axis=0)

def radial_flux(state):
    ion_log, axial_vel, radial_vel, neutral_log, temper = (state[0], state[1], state[2], state[3], state[4])
    return jnp.stack([jnp.exp(ion_log) * radial_vel, axial_vel * radial_vel, 0.5 * radial_vel * radial_vel + temper, 0.5 * jnp.exp(neutral_log) * radial_vel, radial_vel * temper], axis=0)

def source_terms(state):
    axial_vel, radial_vel, neutral_log, temper = (state[1], state[2], state[3], state[4])
    ionize = ionize_rate * jnp.exp(neutral_log) * temper
    return jnp.stack([ionize, field_push * temper - collide_rate * axial_vel, -collide_rate * radial_vel, -ionize, field_push * axial_vel - energy_loss * temper * temper], axis=0)

def numeric_flux(flux, left, right):
    return 0.5 * (flux(left) + flux(right)) - dissipation * (right - left)

def spatial_pieces(extended):
    inner = extended[:, 1:-1]
    axial_faces = numeric_flux(axial_flux, extended[:, :-1], extended[:, 1:])
    padded = jnp.pad(inner, ((0, 0), (0, 0), (1, 1)))
    radial_faces = numeric_flux(radial_flux, padded[:, :, :-1], padded[:, :, 1:])
    radial_div = radial_faces[:, :, :-1] - radial_faces[:, :, 1:]
    return (axial_faces, radial_div, source_terms(inner))

def spatial_adjoint(extended, weighted, source_side):
    _, pullback = jax.vjp(spatial_pieces, extended)
    axial_side = weighted[:, 1:] - weighted[:, :-1]
    cotangent, = pullback((axial_side, weighted[:, 1:-1], source_side))
    return cotangent[:, 1:-1]

def reference(base_state, adjoint, gradient, cell_types):
    fluid = (cell_types != 1).astype(jnp.float32)
    feed = (cell_types == 0).astype(jnp.float32) + 3.0 * (cell_types == 2).astype(jnp.float32)
    wall = (cell_types == 1).astype(jnp.float32)
    wave = jnp.fft.fftfreq(INSTANCES) * INSTANCES
    wave = jnp.where(jnp.arange(INSTANCES) == INSTANCES // 2, 0.0, wave)
    spectrum = jnp.fft.fft(adjoint, axis=0)
    derivative = jnp.real(jnp.fft.ifft(1j * wave[:, None, None, None] * spectrum, axis=0)).astype(jnp.float32)
    time_term = -(time_factor / INSTANCES) * derivative

    def one_instance(pair):
        state, costate = pair
        extended = jnp.pad(state, ((0, 0), (1, 1), (0, 0)))
        weighted = jnp.pad(fluid * costate, ((0, 0), (1, 1), (0, 0)))
        return spatial_adjoint(extended, weighted, feed * costate)
    spatial = lax.map(one_instance, (base_state, adjoint))
    return time_term + spatial - wall_relax * wall * adjoint - gradient
```

```python
import jax
import jax.numpy as jnp
import numpy as np
from jax import lax
from jax.experimental import pallas as pl
from jax.experimental.pallas import tpu as pltpu
from jax.sharding import PartitionSpec as P

dissipation = 0.5
ionize_rate = 0.6
collide_rate = 0.4
energy_loss = 0.3
field_push = 0.8
wall_relax = 2.0
time_factor = 4.0

LANES = 128
SUB = 8


def derivative_matrix(total):
    gap = np.arange(total)[:, None] - np.arange(total)[None, :]
    off = gap != 0
    angle = np.where(off, np.pi * gap / total, 1.0)
    entry = np.where(off, 0.5 * np.where(gap % 2 == 0, 1.0, -1.0) / np.tan(angle), 0.0)
    entry = -(time_factor / total) * entry
    high = entry.astype(jnp.bfloat16)
    low = (entry - high.astype(np.float64)).astype(jnp.bfloat16)
    return np.concatenate([high, high, low], axis=1)


def pack_kernel(chunk, parts, x_ref, o_ref):
    for d in range(parts):
        o_ref[pl.ds(d * chunk, chunk), :] = x_ref[pl.ds(d, chunk, stride=parts), :]


def edge_kernel(x_ref, c_ref, low_ref, high_ref):
    local, fields, axial, _ = x_ref.shape
    for row, o_ref in ((0, low_ref), (axial - 1, high_ref)):
        fluid = (c_ref[row : row + 1, :] != 1).astype(jnp.float32)
        for i in range(local):
            for f in range(fields):
                o_ref[i * fields + f] = fluid * x_ref[i, f, row : row + 1, :]


def spatial_kernel(state_ref, adjoint_ref, gradient_ref, cell_ref, before_ref, after_ref, o_ref):
    local, fields, axial, radial = state_ref.shape
    cell = cell_ref[...]
    fluid = (cell != 1).astype(jnp.float32)
    feed = (cell == 0).astype(jnp.float32) + 3.0 * (cell == 2).astype(jnp.float32)
    relax = wall_relax * (cell == 1).astype(jnp.float32)
    row = lax.broadcasted_iota(jnp.int32, (axial, radial), 0)
    lane = lax.broadcasted_iota(jnp.int32, (axial, radial), 1)
    for i in range(local):
        axial_diff, radial_diff, source, spread = [], [], [], []
        for f in range(fields):
            adjoint = adjoint_ref[i, f]
            weighted = fluid * adjoint
            before = jnp.where(row == 0, before_ref[i * fields + f], pltpu.roll(weighted, 1, 0))
            after = jnp.where(
                row == axial - 1, after_ref[i * fields + f], pltpu.roll(weighted, axial - 1, 0)
            )
            inward = jnp.where(lane == 0, 0.0, pltpu.roll(weighted, 1, 1))
            outward = jnp.where(lane == radial - 1, 0.0, pltpu.roll(weighted, radial - 1, 1))
            axial_diff.append(0.5 * (after - before))
            radial_diff.append(0.5 * (outward - inward))
            source.append(feed * adjoint)
            spread.append(
                dissipation * ((after + before) + (outward + inward))
                - (4.0 * dissipation) * weighted
                - relax * adjoint
                - gradient_ref[i, f]
            )
        ion = jnp.exp(state_ref[i, 0])
        u = state_ref[i, 1]
        v = state_ref[i, 2]
        neutral = jnp.exp(state_ref[i, 3])
        temper = state_ref[i, 4]
        p, q, m = axial_diff, radial_diff, source
        ionize = ionize_rate * neutral * (m[0] - m[3])
        o_ref[i, 0] = spread[0] + ion * (u * p[0] + v * q[0])
        o_ref[i, 1] = (
            spread[1]
            + (ion * p[0] + u * p[1] + v * (p[2] + q[1]) + temper * p[4])
            + (field_push * m[4] - collide_rate * m[1])
        )
        o_ref[i, 2] = (
            spread[2]
            + (ion * q[0] + u * (p[2] + q[1]) + v * q[2] + 0.5 * neutral * q[3] + temper * q[4])
            - collide_rate * m[2]
        )
        o_ref[i, 3] = spread[3] + neutral * (p[3] + 0.5 * v * q[3]) + ionize * temper
        o_ref[i, 4] = (
            spread[4]
            + (p[1] + q[2] + u * p[4] + v * q[4])
            + (ionize + field_push * m[1] - (2.0 * energy_loss) * temper * m[4])
        )


def product_kernel(fields, total, d_ref, x_ref, o_ref):
    columns = jnp.concatenate(
        [x_ref[pl.ds(f, total, stride=fields), :] for f in range(fields)], axis=1
    )
    high = columns.astype(jnp.bfloat16)
    low = (columns - high.astype(jnp.float32)).astype(jnp.bfloat16)
    stacked = jnp.concatenate([high, low, high], axis=0)
    result = jnp.dot(d_ref[...], stacked, preferred_element_type=jnp.float32)
    for f in range(fields):
        o_ref[pl.ds(f, total, stride=fields), :] = result[:, f * LANES : (f + 1) * LANES]


def combine_kernel(chunk, parts, t_ref, s_ref, o_ref):
    for q in range(chunk):
        rows = pl.ds(q * parts, parts)
        o_ref[rows, :] = t_ref[pl.ds(q, parts, stride=chunk), :] + s_ref[rows, :]


def to_tiles(x):
    local, fields, axial, radial = x.shape
    x = x.reshape(local, fields, axial // SUB, SUB, radial // LANES, LANES)
    return x.transpose(0, 1, 2, 4, 3, 5).reshape(-1, LANES)


def from_tiles(x, shape):
    local, fields, axial, radial = shape
    x = x.reshape(local, fields, axial // SUB, radial // LANES, SUB, LANES)
    return x.transpose(0, 1, 2, 4, 3, 5).reshape(shape)


def per_device(base_state, adjoint, gradient, cell_types):
    shape = adjoint.shape
    local, fields, _, radial = shape
    parts = lax.axis_size("inst")
    total = local * parts
    chunk = local * fields
    rows = adjoint.size // LANES
    space = pl.BlockSpec(memory_space=pltpu.VMEM)

    def run(kernel, name, outs, *operands, flops=0):
        single = isinstance(outs, tuple)
        shapes = [jax.ShapeDtypeStruct(s, jnp.float32) for s in ([outs] if single else outs)]
        moved = sum(x.size for x in operands) + sum(s.size for s in shapes)
        return pl.pallas_call(
            kernel,
            out_shape=shapes[0] if single else shapes,
            in_specs=[space] * len(operands),
            out_specs=space if single else [space] * len(shapes),
            name=name,
            cost_estimate=pl.CostEstimate(
                flops=flops, bytes_accessed=4 * moved, transcendentals=0
            ),
        )(*operands)

    def exchange(x):
        x = x.reshape(parts, fields, local, LANES)
        return lax.all_to_all(x, "inst", 0, 0).reshape(rows, LANES)

    flat = (rows, LANES)
    packed = run(lambda *r: pack_kernel(chunk, parts, *r), "pack", flat, to_tiles(adjoint))
    columns = exchange(packed)
    product = run(
        lambda *r: product_kernel(fields, total, *r),
        "time_product",
        flat,
        jnp.asarray(derivative_matrix(total)),
        columns,
        flops=6 * total * total * fields * LANES,
    )
    time_part = exchange(product)

    edge = (chunk, 1, radial)
    first, last = run(edge_kernel, "edges", [edge, edge], adjoint, cell_types)
    count = lax.axis_size("space")
    up = [(i, i + 1) for i in range(count - 1)]
    down = [(i + 1, i) for i in range(count - 1)]
    before = lax.ppermute(last, "space", up)
    after = lax.ppermute(first, "space", down)
    rest = run(
        spatial_kernel,
        "spatial",
        shape,
        base_state,
        adjoint,
        gradient,
        cell_types,
        before,
        after,
        flops=60 * adjoint.size,
    )
    out = run(
        lambda *r: combine_kernel(chunk, parts, *r), "combine", flat, time_part, to_tiles(rest)
    )
    return from_tiles(out, shape)


def solution(mesh):
    return jax.shard_map(
        per_device,
        mesh=mesh,
        in_specs=(
            P("inst", None, "space", None),
            P("inst", None, "space", None),
            P("inst", None, "space", None),
            P("space", None),
        ),
        out_specs=P("inst", None, "space", None),
        check_vma=False,
    )
```

```python
import jax
import jax.numpy as jnp
import numpy as np
from jax import lax
from jax.experimental import pallas as pl
from jax.experimental.pallas import tpu as pltpu
from jax.sharding import PartitionSpec as P

dissipation = 0.5
ionize_rate = 0.6
collide_rate = 0.4
energy_loss = 0.3
field_push = 0.8
wall_relax = 2.0
time_factor = 4.0

LANES = 128
SUB = 8


def derivative_matrix(total):
    gap = np.arange(total)[:, None] - np.arange(total)[None, :]
    off = gap != 0
    angle = np.where(off, np.pi * gap / total, 1.0)
    entry = np.where(off, 0.5 * np.where(gap % 2 == 0, 1.0, -1.0) / np.tan(angle), 0.0)
    entry = -(time_factor / total) * entry
    high = entry.astype(jnp.bfloat16)
    low = (entry - high.astype(np.float64)).astype(jnp.bfloat16)
    return np.concatenate([high, high, low], axis=1)


def pack_kernel(x_ref, o_ref, held_ref, done_ref):
    groups, chunk, size, _ = held_ref.shape
    copies = [
        pltpu.make_async_copy(x_ref.at[:, pl.ds(g * size, size), :], held_ref.at[g], done_ref.at[g])
        for g in range(groups)
    ]
    for copy in copies:
        copy.start()
    for g in range(groups):
        copies[g].wait()
        rows = held_ref.at[g].reshape(chunk * size, LANES)
        for d in range(size):
            o_ref[pl.ds((g * size + d) * chunk, chunk), :] = rows[pl.ds(d, chunk, stride=size), :]


def edge_kernel(x_ref, c_ref, low_ref, high_ref):
    local, fields, axial, _ = x_ref.shape
    for row, o_ref in ((0, low_ref), (axial - 1, high_ref)):
        fluid = (c_ref[row : row + 1, :] != 1).astype(jnp.float32)
        for i in range(local):
            for f in range(fields):
                o_ref[i * fields + f] = fluid * x_ref[i, f, row : row + 1, :]


def spatial_kernel(state_ref, adjoint_ref, gradient_ref, cell_ref, before_ref, after_ref, o_ref):
    local, fields, axial, radial = state_ref.shape
    cell = cell_ref[...]
    fluid = (cell != 1).astype(jnp.float32)
    feed = (cell == 0).astype(jnp.float32) + 3.0 * (cell == 2).astype(jnp.float32)
    relax = wall_relax * (cell == 1).astype(jnp.float32)
    row = lax.broadcasted_iota(jnp.int32, (axial, radial), 0)
    lane = lax.broadcasted_iota(jnp.int32, (axial, radial), 1)
    for i in range(local):
        axial_diff, radial_diff, source, spread = [], [], [], []
        for f in range(fields):
            adjoint = adjoint_ref[i, f]
            weighted = fluid * adjoint
            before = jnp.where(row == 0, before_ref[i * fields + f], pltpu.roll(weighted, 1, 0))
            after = jnp.where(
                row == axial - 1, after_ref[i * fields + f], pltpu.roll(weighted, axial - 1, 0)
            )
            inward = jnp.where(lane == 0, 0.0, pltpu.roll(weighted, 1, 1))
            outward = jnp.where(lane == radial - 1, 0.0, pltpu.roll(weighted, radial - 1, 1))
            axial_diff.append(0.5 * (after - before))
            radial_diff.append(0.5 * (outward - inward))
            source.append(feed * adjoint)
            spread.append(
                dissipation * ((after + before) + (outward + inward))
                - (4.0 * dissipation) * weighted
                - relax * adjoint
                - gradient_ref[i, f]
            )
        ion = jnp.exp(state_ref[i, 0])
        u = state_ref[i, 1]
        v = state_ref[i, 2]
        neutral = jnp.exp(state_ref[i, 3])
        temper = state_ref[i, 4]
        p, q, m = axial_diff, radial_diff, source
        ionize = ionize_rate * neutral * (m[0] - m[3])
        o_ref[i, 0] = spread[0] + ion * (u * p[0] + v * q[0])
        o_ref[i, 1] = (
            spread[1]
            + (ion * p[0] + u * p[1] + v * (p[2] + q[1]) + temper * p[4])
            + (field_push * m[4] - collide_rate * m[1])
        )
        o_ref[i, 2] = (
            spread[2]
            + (ion * q[0] + u * (p[2] + q[1]) + v * q[2] + 0.5 * neutral * q[3] + temper * q[4])
            - collide_rate * m[2]
        )
        o_ref[i, 3] = spread[3] + neutral * (p[3] + 0.5 * v * q[3]) + ionize * temper
        o_ref[i, 4] = (
            spread[4]
            + (p[1] + q[2] + u * p[4] + v * q[4])
            + (ionize + field_push * m[1] - (2.0 * energy_loss) * temper * m[4])
        )


def product_kernel(fields, total, d_ref, x_ref, o_ref):
    columns = jnp.concatenate(
        [x_ref[pl.ds(f, total, stride=fields), :] for f in range(fields)], axis=1
    )
    high = columns.astype(jnp.bfloat16)
    low = (columns - high.astype(jnp.float32)).astype(jnp.bfloat16)
    stacked = jnp.concatenate([high, low, high], axis=0)
    result = jnp.dot(d_ref[...], stacked, preferred_element_type=jnp.float32)
    for f in range(fields):
        o_ref[pl.ds(f, total, stride=fields), :] = result[:, f * LANES : (f + 1) * LANES]


def combine_kernel(chunk, t_ref, s_ref, o_ref, held_ref, done_ref):
    groups, size, _ = held_ref.shape
    parts = groups * size // chunk
    copies = []
    for g in range(groups):
        for q in range(size // parts):
            tile = g * (size // parts) + q
            held_ref[g, pl.ds(q * parts, parts), :] = (
                t_ref[pl.ds(tile, parts, stride=chunk), :] + s_ref[pl.ds(tile * parts, parts), :]
            )
        copies.append(
            pltpu.make_async_copy(
                held_ref.at[g], o_ref.at[pl.ds(g * size, size), :], done_ref.at[g]
            )
        )
        copies[g].start()
    for copy in copies:
        copy.wait()


def to_tiles(x):
    local, fields, axial, radial = x.shape
    x = x.reshape(local, fields, axial // SUB, SUB, radial // LANES, LANES)
    return x.transpose(0, 1, 2, 4, 3, 5).reshape(-1, LANES)


def from_tiles(x, shape):
    local, fields, axial, radial = shape
    x = x.reshape(local, fields, axial // SUB, radial // LANES, SUB, LANES)
    return x.transpose(0, 1, 2, 4, 3, 5).reshape(shape)


def per_device(base_state, adjoint, gradient, cell_types):
    shape = adjoint.shape
    local, fields, _, radial = shape
    parts = lax.axis_size("inst")
    total = local * parts
    chunk = local * fields
    rows = adjoint.size // LANES
    far = pl.BlockSpec(memory_space=pl.ANY)
    near = pl.BlockSpec(memory_space=pltpu.VMEM)
    resident = "resident"

    def run(kernel, name, outs, ins, *operands, scratch=(), flops=0):
        moved = sum(x.size for x in operands) + sum(o.size for o, _ in outs)
        operands = [
            pltpu.with_memory_space_constraint(x, pltpu.VMEM) if m is resident else x
            for x, m in zip(operands, ins)
        ]
        shapes = [
            pltpu.VMEM(o.shape, jnp.float32) if m is resident else o for o, m in outs
        ]
        specs = [far if m is far else near for _, m in outs]
        return pl.pallas_call(
            kernel,
            out_shape=shapes if len(shapes) > 1 else shapes[0],
            in_specs=[far if m is far else near for m in ins],
            out_specs=specs if len(specs) > 1 else specs[0],
            scratch_shapes=list(scratch),
            name=name,
            cost_estimate=pl.CostEstimate(
                flops=flops, bytes_accessed=4 * moved, transcendentals=0
            ),
        )(*operands)

    def exchange(x):
        x = x.reshape(parts, fields, local, LANES)
        return lax.all_to_all(x, "inst", 0, 0).reshape(rows, LANES)

    flat = jax.ShapeDtypeStruct((rows, LANES), jnp.float32)
    groups = parts // SUB
    packed = run(
        pack_kernel,
        "pack",
        [(flat, resident)],
        [far],
        to_tiles(adjoint).reshape(chunk, parts, LANES),
        scratch=[
            pltpu.VMEM((groups, chunk, SUB, LANES), jnp.float32),
            pltpu.SemaphoreType.DMA((groups,)),
        ],
    )
    columns = exchange(packed)
    product = run(
        lambda *r: product_kernel(fields, total, *r),
        "time_product",
        [(flat, resident)],
        [resident, resident],
        jnp.asarray(derivative_matrix(total)),
        columns,
        flops=6 * total * total * fields * LANES,
    )
    time_part = exchange(product)

    edge = jax.ShapeDtypeStruct((chunk, 1, radial), jnp.float32)
    first, last = run(
        edge_kernel, "edges", [(edge, near), (edge, near)], [near, near], adjoint, cell_types
    )
    count = lax.axis_size("space")
    up = [(i, i + 1) for i in range(count - 1)]
    down = [(i + 1, i) for i in range(count - 1)]
    before = lax.ppermute(last, "space", up)
    after = lax.ppermute(first, "space", down)
    rest = run(
        spatial_kernel,
        "spatial",
        [(jax.ShapeDtypeStruct(shape, jnp.float32), resident)],
        [near] * 6,
        base_state,
        adjoint,
        gradient,
        cell_types,
        before,
        after,
        flops=60 * adjoint.size,
    )
    pieces = fields
    out = run(
        lambda *r: combine_kernel(chunk, *r),
        "combine",
        [(flat, far)],
        [resident, resident],
        time_part,
        to_tiles(rest),
        scratch=[
            pltpu.VMEM((pieces, rows // pieces, LANES), jnp.float32),
            pltpu.SemaphoreType.DMA((pieces,)),
        ],
    )
    return from_tiles(out, shape)


def solution(mesh):
    return jax.shard_map(
        per_device,
        mesh=mesh,
        in_specs=(
            P("inst", None, "space", None),
            P("inst", None, "space", None),
            P("inst", None, "space", None),
            P("space", None),
        ),
        out_specs=P("inst", None, "space", None),
        check_vma=False,
    )
```

```python
import jax
import jax.numpy as jnp
import numpy as np
from jax import lax
from jax.experimental import pallas as pl
from jax.experimental.pallas import tpu as pltpu
from jax.sharding import PartitionSpec as P

dissipation = 0.5
ionize_rate = 0.6
collide_rate = 0.4
energy_loss = 0.3
field_push = 0.8
wall_relax = 2.0
time_factor = 4.0

LANES = 128
SUB = 8
FIRST_PART = 43


def derivative_matrix(total):
    gap = np.arange(total)[:, None] - np.arange(total)[None, :]
    off = gap != 0
    angle = np.where(off, np.pi * gap / total, 1.0)
    entry = np.where(off, 0.5 * np.where(gap % 2 == 0, 1.0, -1.0) / np.tan(angle), 0.0)
    entry = -(time_factor / total) * entry
    high = entry.astype(jnp.bfloat16)
    low = (entry - high.astype(np.float64)).astype(jnp.bfloat16)
    return np.concatenate([high, high, low], axis=1)


def pack_kernel(across, x_ref, cell_ref, o_ref, edge_ref, held_ref, kinds_ref, done_ref, told_ref):
    groups, chunk, size, _ = held_ref.shape
    copies = [
        pltpu.make_async_copy(x_ref.at[:, pl.ds(g * size, size), :], held_ref.at[g], done_ref.at[g])
        for g in range(groups)
    ]
    tell = pltpu.make_async_copy(cell_ref, kinds_ref, told_ref)
    for copy in copies:
        copy.start()
    tell.start()
    for g in range(groups):
        copies[g].wait()
        rows = held_ref.at[g].reshape(chunk * size, LANES)
        for d in range(size):
            o_ref[pl.ds((g * size + d) * chunk, chunk), :] = rows[pl.ds(d, chunk, stride=size), :]
    tell.wait()
    for side, (first, row) in enumerate(((0, 0), (groups - across, size - 1))):
        for c in range(across):
            fluid = (kinds_ref[first + c, row : row + 1, :] != 1).astype(jnp.float32)
            place = ((first + c) * size + row) * chunk
            edge_ref[side, c] = fluid * o_ref[pl.ds(place, chunk), :]


def spatial_kernel(me_ref, edge_ref, state_ref, adjoint_ref, gradient_ref, cell_ref, o_ref):
    me = me_ref[0]
    count, _, across, _, _ = edge_ref.shape
    below, above = jnp.maximum(me - 1, 0), jnp.minimum(me + 1, count - 1)
    has_below = (me > 0).astype(jnp.float32)
    has_above = (me < count - 1).astype(jnp.float32)

    def beyond(member, side, q):
        return jnp.concatenate(
            [edge_ref[member, side, c, q : q + 1, :] for c in range(across)], axis=1
        )

    local, fields, axial, radial = state_ref.shape
    cell = cell_ref[...]
    fluid = (cell != 1).astype(jnp.float32)
    feed = (cell == 0).astype(jnp.float32) + 3.0 * (cell == 2).astype(jnp.float32)
    relax = wall_relax * (cell == 1).astype(jnp.float32)
    row = lax.broadcasted_iota(jnp.int32, (axial, radial), 0)
    lane = lax.broadcasted_iota(jnp.int32, (axial, radial), 1)
    for i in range(local):
        axial_diff, radial_diff, source, spread = [], [], [], []
        for f in range(fields):
            adjoint = adjoint_ref[i, f]
            weighted = fluid * adjoint
            q = i * fields + f
            before = jnp.where(
                row == 0, has_below * beyond(below, 1, q), pltpu.roll(weighted, 1, 0)
            )
            after = jnp.where(
                row == axial - 1,
                has_above * beyond(above, 0, q),
                pltpu.roll(weighted, axial - 1, 0),
            )
            inward = jnp.where(lane == 0, 0.0, pltpu.roll(weighted, 1, 1))
            outward = jnp.where(lane == radial - 1, 0.0, pltpu.roll(weighted, radial - 1, 1))
            axial_diff.append(0.5 * (after - before))
            radial_diff.append(0.5 * (outward - inward))
            source.append(feed * adjoint)
            spread.append(
                dissipation * ((after + before) + (outward + inward))
                - (4.0 * dissipation) * weighted
                - relax * adjoint
                - gradient_ref[i, f]
            )
        ion = jnp.exp(state_ref[i, 0])
        u = state_ref[i, 1]
        v = state_ref[i, 2]
        neutral = jnp.exp(state_ref[i, 3])
        temper = state_ref[i, 4]
        p, q, m = axial_diff, radial_diff, source
        ionize = ionize_rate * neutral * (m[0] - m[3])
        o_ref[i, 0] = spread[0] + ion * (u * p[0] + v * q[0])
        o_ref[i, 1] = (
            spread[1]
            + (ion * p[0] + u * p[1] + v * (p[2] + q[1]) + temper * p[4])
            + (field_push * m[4] - collide_rate * m[1])
        )
        o_ref[i, 2] = (
            spread[2]
            + (ion * q[0] + u * (p[2] + q[1]) + v * q[2] + 0.5 * neutral * q[3] + temper * q[4])
            - collide_rate * m[2]
        )
        o_ref[i, 3] = spread[3] + neutral * (p[3] + 0.5 * v * q[3]) + ionize * temper
        o_ref[i, 4] = (
            spread[4]
            + (p[1] + q[2] + u * p[4] + v * q[4])
            + (ionize + field_push * m[1] - (2.0 * energy_loss) * temper * m[4])
        )


def product_kernel(fields, total, d_ref, x_ref, o_ref):
    columns = jnp.concatenate(
        [x_ref[pl.ds(f, total, stride=fields), :] for f in range(fields)], axis=1
    )
    high = columns.astype(jnp.bfloat16)
    low = (columns - high.astype(jnp.float32)).astype(jnp.bfloat16)
    stacked = jnp.concatenate([high, low, high], axis=0)
    result = jnp.dot(d_ref[...], stacked, preferred_element_type=jnp.float32)
    for f in range(fields):
        o_ref[pl.ds(f, total, stride=fields), :] = result[:, f * LANES : (f + 1) * LANES]


def combine_kernel(chunk, t_ref, s_ref, o_ref, held_ref, done_ref):
    groups, size, _ = held_ref.shape
    parts = groups * size // chunk
    copies = []
    for g in range(groups):
        for q in range(size // parts):
            tile = g * (size // parts) + q
            held_ref[g, pl.ds(q * parts, parts), :] = (
                t_ref[pl.ds(tile, parts, stride=chunk), :] + s_ref[pl.ds(tile * parts, parts), :]
            )
        copies.append(
            pltpu.make_async_copy(
                held_ref.at[g], o_ref.at[pl.ds(g * size, size), :], done_ref.at[g]
            )
        )
        copies[g].start()
    for copy in copies:
        copy.wait()


def to_tiles(x):
    local, fields, axial, radial = x.shape
    x = x.reshape(local, fields, axial // SUB, SUB, radial // LANES, LANES)
    return x.transpose(0, 1, 2, 4, 3, 5).reshape(-1, LANES)


def from_tiles(x, shape):
    local, fields, axial, radial = shape
    x = x.reshape(local, fields, axial // SUB, radial // LANES, SUB, LANES)
    return x.transpose(0, 1, 2, 4, 3, 5).reshape(shape)


def per_device(base_state, adjoint, gradient, cell_types):
    shape = adjoint.shape
    local, fields, _, radial = shape
    parts = lax.axis_size("inst")
    total = local * parts
    chunk = local * fields
    rows = adjoint.size // LANES
    far = pl.BlockSpec(memory_space=pl.ANY)
    near = pl.BlockSpec(memory_space=pltpu.VMEM)
    scalars = pl.BlockSpec(memory_space=pltpu.SMEM)
    resident = "resident"

    def run(kernel, name, outs, ins, *operands, scratch=(), flops=0):
        moved = sum(x.size for x in operands) + sum(o.size for o, _ in outs)
        operands = [
            pltpu.with_memory_space_constraint(x, pltpu.VMEM) if m is resident else x
            for x, m in zip(operands, ins)
        ]
        shapes = [
            pltpu.VMEM(o.shape, jnp.float32) if m is resident else o for o, m in outs
        ]
        specs = [far if m is far else near for _, m in outs]
        return pl.pallas_call(
            kernel,
            out_shape=shapes if len(shapes) > 1 else shapes[0],
            in_specs=[near if m is resident else m for m in ins],
            out_specs=specs if len(specs) > 1 else specs[0],
            scratch_shapes=list(scratch),
            name=name,
            cost_estimate=pl.CostEstimate(
                flops=flops, bytes_accessed=4 * moved, transcendentals=0
            ),
        )(*operands)

    def exchange(x):
        x = x.reshape(parts, fields, local, LANES)
        return lax.all_to_all(x, "inst", 0, 0, axis_index_groups=[order]).reshape(rows, LANES)

    first_part = FIRST_PART % parts
    order = [(first_part + p) % parts for p in range(parts)]
    flat = jax.ShapeDtypeStruct((rows, LANES), jnp.float32)
    groups = parts // SUB
    across = radial // LANES
    kinds = cell_types.reshape(-1, SUB, across, LANES).transpose(0, 2, 1, 3)
    edge = jax.ShapeDtypeStruct((2, across, chunk, LANES), jnp.float32)
    packed, edges = run(
        lambda *r: pack_kernel(across, *r),
        "pack",
        [(flat, resident), (edge, resident)],
        [far, far],
        to_tiles(adjoint).reshape(chunk, parts, LANES),
        kinds.reshape(groups, SUB, LANES),
        scratch=[
            pltpu.VMEM((groups, chunk, SUB, LANES), jnp.float32),
            pltpu.VMEM((groups, SUB, LANES), jnp.int32),
            pltpu.SemaphoreType.DMA((groups,)),
            pltpu.SemaphoreType.DMA,
        ],
    )
    all_edges = lax.all_gather(edges, "space")
    columns = exchange(packed)
    product = run(
        lambda *r: product_kernel(fields, total, *r),
        "time_product",
        [(flat, resident)],
        [resident, resident],
        jnp.asarray(derivative_matrix(total)),
        columns,
        flops=6 * total * total * fields * LANES,
    )
    time_part = exchange(product)

    rest = run(
        spatial_kernel,
        "spatial",
        [(jax.ShapeDtypeStruct(shape, jnp.float32), resident)],
        [scalars] + [near] * 5,
        lax.axis_index("space").astype(jnp.int32).reshape(1),
        all_edges,
        base_state,
        adjoint,
        gradient,
        cell_types,
        flops=60 * adjoint.size,
    )
    pieces = fields
    out = run(
        lambda *r: combine_kernel(chunk, *r),
        "combine",
        [(flat, far)],
        [resident, resident],
        time_part,
        to_tiles(rest),
        scratch=[
            pltpu.VMEM((pieces, rows // pieces, LANES), jnp.float32),
            pltpu.SemaphoreType.DMA((pieces,)),
        ],
    )
    return from_tiles(out, shape)


def solution(mesh):
    return jax.shard_map(
        per_device,
        mesh=mesh,
        in_specs=(
            P("inst", None, "space", None),
            P("inst", None, "space", None),
            P("inst", None, "space", None),
            P("space", None),
        ),
        out_specs=P("inst", None, "space", None),
        check_vma=False,
    )
```

```python
import jax
import jax.numpy as jnp
import numpy as np
from jax import lax
from jax.experimental import pallas as pl
from jax.experimental.pallas import tpu as pltpu
from jax.sharding import PartitionSpec as P

dissipation = 0.5
ionize_rate = 0.6
collide_rate = 0.4
energy_loss = 0.3
field_push = 0.8
wall_relax = 2.0
time_factor = 4.0

LANES = 128
SUB = 8
FIRST_PART = 43


def derivative_matrix(total):
    gap = np.arange(total)[:, None] - np.arange(total)[None, :]
    off = gap != 0
    angle = np.where(off, np.pi * gap / total, 1.0)
    entry = np.where(off, 0.5 * np.where(gap % 2 == 0, 1.0, -1.0) / np.tan(angle), 0.0)
    entry = -(time_factor / total) * entry
    high = entry.astype(jnp.bfloat16)
    low = (entry - high.astype(np.float64)).astype(jnp.bfloat16)
    return np.concatenate([high, high, low], axis=1)


def interior(
    state_ref, adjoint_ref, gradient_ref, cell_ref, out_ref,
    held_refs, o_ref, held_cell, done_ref, out_done, told,
):
    local, fields, axial, radial = out_ref.shape
    def fetch(i):
        return [
            pltpu.make_async_copy(far_ref.at[i], near_ref.at[i % 2], done_ref.at[i % 2, n])
            for n, (far_ref, near_ref) in enumerate(
                zip((state_ref, adjoint_ref, gradient_ref), held_refs)
            )
        ]

    for copy in fetch(0):
        copy.start()
    kinds = pltpu.make_async_copy(cell_ref, held_cell, told)
    kinds.start()
    kinds.wait()
    cell = held_cell[...]
    fluid = (cell != 1).astype(jnp.float32)
    feed = (cell == 0).astype(jnp.float32) + 3.0 * (cell == 2).astype(jnp.float32)
    relax = wall_relax * (cell == 1).astype(jnp.float32)
    row = lax.broadcasted_iota(jnp.int32, (axial, radial), 0)
    lane = lax.broadcasted_iota(jnp.int32, (axial, radial), 1)
    for i in range(local):
        for copy in fetch(i):
            copy.wait()
        if i + 1 < local:
            for copy in fetch(i + 1):
                copy.start()
        held_state, held_adjoint, held_gradient = (ref.at[i % 2] for ref in held_refs)
        axial_diff, radial_diff, source, spread = [], [], [], []
        for f in range(fields):
            adjoint = held_adjoint[f]
            weighted = fluid * adjoint
            before = jnp.where(row == 0, 0.0, pltpu.roll(weighted, 1, 0))
            after = jnp.where(row == axial - 1, 0.0, pltpu.roll(weighted, axial - 1, 0))
            inward = jnp.where(lane == 0, 0.0, pltpu.roll(weighted, 1, 1))
            outward = jnp.where(lane == radial - 1, 0.0, pltpu.roll(weighted, radial - 1, 1))
            axial_diff.append(0.5 * (after - before))
            radial_diff.append(0.5 * (outward - inward))
            source.append(feed * adjoint)
            spread.append(
                dissipation * ((after + before) + (outward + inward))
                - (4.0 * dissipation) * weighted
                - relax * adjoint
                - held_gradient[f]
            )
        ion = jnp.exp(held_state[0])
        u = held_state[1]
        v = held_state[2]
        neutral = jnp.exp(held_state[3])
        temper = held_state[4]
        p, q, m = axial_diff, radial_diff, source
        ionize = ionize_rate * neutral * (m[0] - m[3])
        if i > 0:
            out.wait()
        o_ref[0] = spread[0] + ion * (u * p[0] + v * q[0])
        o_ref[1] = (
            spread[1]
            + (ion * p[0] + u * p[1] + v * (p[2] + q[1]) + temper * p[4])
            + (field_push * m[4] - collide_rate * m[1])
        )
        o_ref[2] = (
            spread[2]
            + (ion * q[0] + u * (p[2] + q[1]) + v * q[2] + 0.5 * neutral * q[3] + temper * q[4])
            - collide_rate * m[2]
        )
        o_ref[3] = spread[3] + neutral * (p[3] + 0.5 * v * q[3]) + ionize * temper
        o_ref[4] = (
            spread[4]
            + (p[1] + q[2] + u * p[4] + v * q[4])
            + (ionize + field_push * m[1] - (2.0 * energy_loss) * temper * m[4])
        )
        out = pltpu.make_async_copy(o_ref, out_ref.at[i], out_done)
        out.start()
    out.wait()


def pack_kernel(
    across, me_ref, x_ref, kind_ref, state_ref, adjoint_ref, gradient_ref, cell_ref,
    o_ref, edge_ref, rest_ref,
    held_ref, kinds_ref, done_ref, told_ref, *work,
):
    groups, chunk, size, _ = held_ref.shape

    copies = [
        pltpu.make_async_copy(x_ref.at[:, pl.ds(g * size, size), :], held_ref.at[g], done_ref.at[g])
        for g in range(groups)
    ]
    tell = pltpu.make_async_copy(kind_ref, kinds_ref, told_ref)
    for copy in copies:
        copy.start()
    tell.start()
    @pl.when(me_ref[0] % 2 == 0)
    def _():
        interior(
            state_ref, adjoint_ref, gradient_ref, cell_ref, rest_ref, work[:3], *work[3:]
        )

    for g in range(groups):
        copies[g].wait()
        rows = held_ref.at[g].reshape(chunk * size, LANES)
        for d in range(size):
            o_ref[pl.ds((g * size + d) * chunk, chunk), :] = rows[pl.ds(d, chunk, stride=size), :]
    tell.wait()
    for side, (first, row) in enumerate(((0, 0), (groups - across, size - 1))):
        for c in range(across):
            fluid = (kinds_ref[first + c, row : row + 1, :] != 1).astype(jnp.float32)
            place = ((first + c) * size + row) * chunk
            edge_ref[pl.ds((side * across + c) * chunk, chunk), :] = (
                fluid * o_ref[pl.ds(place, chunk), :]
            )


def interior_kernel(
    me_ref, early_ref, edge_ref, state_ref, adjoint_ref, gradient_ref, cell_ref,
    rest_ref, edges_ref, *work,
):
    del early_ref, edge_ref, edges_ref

    @pl.when(me_ref[0] % 2 == 1)
    def _():
        interior(
            state_ref, adjoint_ref, gradient_ref, cell_ref, rest_ref, work[:3], *work[3:]
        )


def border_kernel(before_ref, after_ref, state_ref, o_ref):
    local, fields, axial, radial = state_ref.shape
    across, chunk = radial // LANES, local * fields
    sides = ((0, -0.5, before_ref), (axial - 1, 0.5, after_ref))
    for mine, (row, sign, edge_ref) in enumerate(sides):
        for c in range(across):
            lanes = pl.ds(c * LANES, LANES)
            edges = [
                edge_ref[pl.ds(c * chunk + f, local, stride=fields), :] for f in range(fields)
            ]
            ion, u, v, neutral, temper = [state_ref[:, f, row, lanes] for f in range(fields)]
            ion, neutral = jnp.exp(ion), jnp.exp(neutral)
            p = [sign * e for e in edges]
            added = (
                ion * u * p[0],
                ion * p[0] + u * p[1] + v * p[2] + temper * p[4],
                u * p[2],
                neutral * p[3],
                p[1] + u * p[4],
            )
            for f in range(fields):
                total = dissipation * edges[f] + added[f]
                for i in range(local):
                    o_ref[mine, i * fields + f, c : c + 1, :] = total[i : i + 1, :]


def product_kernel(fields, total, d_ref, x_ref, o_ref):
    columns = jnp.concatenate(
        [x_ref[pl.ds(f, total, stride=fields), :] for f in range(fields)], axis=1
    )
    high = columns.astype(jnp.bfloat16)
    low = (columns - high.astype(jnp.float32)).astype(jnp.bfloat16)
    stacked = jnp.concatenate([high, low, high], axis=0)
    result = jnp.dot(d_ref[...], stacked, preferred_element_type=jnp.float32)
    for f in range(fields):
        o_ref[pl.ds(f, total, stride=fields), :] = result[:, f * LANES : (f + 1) * LANES]


def combine_kernel(chunk, t_ref, s_ref, b_ref, o_ref, held_ref, done_ref):
    groups, size, _ = held_ref.shape
    parts = groups * size // chunk
    copies = []
    for g in range(groups):
        for q in range(size // parts):
            tile = g * (size // parts) + q
            held_ref[g, pl.ds(q * parts, parts), :] = (
                t_ref[pl.ds(tile, parts, stride=chunk), :] + s_ref[pl.ds(tile * parts, parts), :]
            )
            across = b_ref.shape[2]
            for side, at in ((0, 0), (1, parts - across * SUB + SUB - 1)):
                held_ref[g, pl.ds(q * parts + at, across, stride=SUB), :] += b_ref[side, tile]
        copies.append(
            pltpu.make_async_copy(
                held_ref.at[g], o_ref.at[pl.ds(g * size, size), :], done_ref.at[g]
            )
        )
        copies[g].start()
    for copy in copies:
        copy.wait()


def to_tiles(x):
    local, fields, axial, radial = x.shape
    x = x.reshape(local, fields, axial // SUB, SUB, radial // LANES, LANES)
    return x.transpose(0, 1, 2, 4, 3, 5).reshape(-1, LANES)


def from_tiles(x, shape):
    local, fields, axial, radial = shape
    x = x.reshape(local, fields, axial // SUB, radial // LANES, SUB, LANES)
    return x.transpose(0, 1, 2, 4, 3, 5).reshape(shape)


def per_device(base_state, adjoint, gradient, cell_types):
    shape = adjoint.shape
    local, fields, _, radial = shape
    parts = lax.axis_size("inst")
    total = local * parts
    chunk = local * fields
    rows = adjoint.size // LANES
    far = pl.BlockSpec(memory_space=pl.ANY)
    near = pl.BlockSpec(memory_space=pltpu.VMEM)
    scalars = pl.BlockSpec(memory_space=pltpu.SMEM)
    resident = "resident"

    def run(kernel, name, outs, ins, *operands, scratch=(), flops=0, aliases=None):
        moved = sum(x.size for x in operands) + sum(o.size for o, _ in outs)
        operands = [
            pltpu.with_memory_space_constraint(x, pltpu.VMEM) if m is resident else x
            for x, m in zip(operands, ins)
        ]
        shapes = [
            pltpu.VMEM(o.shape, jnp.float32) if m is resident else o for o, m in outs
        ]
        specs = [far if m is far else near for _, m in outs]
        return pl.pallas_call(
            kernel,
            out_shape=shapes if len(shapes) > 1 else shapes[0],
            in_specs=[near if m is resident else m for m in ins],
            out_specs=specs if len(specs) > 1 else specs[0],
            scratch_shapes=list(scratch),
            input_output_aliases=aliases or {},
            name=name,
            cost_estimate=pl.CostEstimate(
                flops=flops, bytes_accessed=4 * moved, transcendentals=0
            ),
        )(*operands)

    def exchange(x):
        x = x.reshape(parts, fields, local, LANES)
        return lax.all_to_all(x, "inst", 0, 0, axis_index_groups=[order]).reshape(rows, LANES)

    first_part = FIRST_PART % parts
    order = [(first_part + p) % parts for p in range(parts)]
    flat = jax.ShapeDtypeStruct((rows, LANES), jnp.float32)
    groups = parts // SUB
    across = radial // LANES
    kinds = cell_types.reshape(-1, SUB, across, LANES).transpose(0, 2, 1, 3)
    edge = jax.ShapeDtypeStruct((2 * across * chunk, LANES), jnp.float32)
    me = lax.axis_index("space").astype(jnp.int32).reshape(1)
    whole = jax.ShapeDtypeStruct(shape, jnp.float32)
    work = [
        *[pltpu.VMEM((2, *shape[1:]), jnp.float32)] * 3,
        pltpu.VMEM(shape[1:], jnp.float32),
        pltpu.VMEM(shape[2:], jnp.int32),
        pltpu.SemaphoreType.DMA((2, 3)),
        pltpu.SemaphoreType.DMA,
        pltpu.SemaphoreType.DMA,
    ]
    packed, edges, early = run(
        lambda *r: pack_kernel(across, *r),
        "pack",
        [(flat, resident), (edge, resident), (whole, far)],
        [scalars] + [far] * 6,
        me,
        to_tiles(adjoint).reshape(chunk, parts, LANES),
        kinds.reshape(groups, SUB, LANES),
        base_state,
        adjoint,
        gradient,
        cell_types,
        scratch=[
            pltpu.VMEM((groups, chunk, SUB, LANES), jnp.float32),
            pltpu.VMEM((groups, SUB, LANES), jnp.int32),
            pltpu.SemaphoreType.DMA((groups,)),
            pltpu.SemaphoreType.DMA,
            *work,
        ],
    )
    columns = exchange(packed)
    product = run(
        lambda *r: product_kernel(fields, total, *r),
        "time_product",
        [(flat, resident)],
        [resident, resident],
        jnp.asarray(derivative_matrix(total)),
        columns,
        flops=6 * total * total * fields * LANES,
    )
    time_part = exchange(product)

    inner, edges = run(
        interior_kernel,
        "interior",
        [(whole, far), (edge, resident)],
        [scalars, far, resident, far, far, far, far],
        me,
        early,
        edges,
        base_state,
        adjoint,
        gradient,
        cell_types,
        scratch=work,
        flops=60 * adjoint.size,
        aliases={1: 0, 2: 1},
    )
    count = lax.axis_size("space")
    half = across * chunk
    up = [(i, i + 1) for i in range(count - 1)]
    down = [(i + 1, i) for i in range(count - 1)]
    borders = run(
        border_kernel,
        "border",
        [(jax.ShapeDtypeStruct((2, chunk, across, LANES), jnp.float32), resident)],
        [resident] * 3,
        lax.ppermute(edges[half:], "space", up),
        lax.ppermute(edges[:half], "space", down),
        base_state,
        flops=4 * adjoint.size,
    )
    pieces = fields
    out = run(
        lambda *r: combine_kernel(chunk, *r),
        "combine",
        [(flat, far)],
        [resident, resident, resident],
        time_part,
        to_tiles(inner),
        borders,
        scratch=[
            pltpu.VMEM((pieces, rows // pieces, LANES), jnp.float32),
            pltpu.SemaphoreType.DMA((pieces,)),
        ],
    )
    return from_tiles(out, shape)


def solution(mesh):
    return jax.shard_map(
        per_device,
        mesh=mesh,
        in_specs=(
            P("inst", None, "space", None),
            P("inst", None, "space", None),
            P("inst", None, "space", None),
            P("space", None),
        ),
        out_specs=P("inst", None, "space", None),
        check_vma=False,
    )
```

```python
import jax
import jax.numpy as jnp
import numpy as np
from jax import lax
from jax.experimental import pallas as pl
from jax.experimental.pallas import tpu as pltpu
from jax.sharding import PartitionSpec as P

dissipation = 0.5
ionize_rate = 0.6
collide_rate = 0.4
energy_loss = 0.3
field_push = 0.8
wall_relax = 2.0
time_factor = 4.0

LANES = 128
SUB = 8
FIRST_PART = 47


def derivative_matrix(total):
    gap = np.arange(total)[:, None] - np.arange(total)[None, :]
    off = gap != 0
    angle = np.where(off, np.pi * gap / total, 1.0)
    entry = np.where(off, 0.5 * np.where(gap % 2 == 0, 1.0, -1.0) / np.tan(angle), 0.0)
    entry = -(time_factor / total) * entry
    high = entry.astype(jnp.bfloat16)
    low = (entry - high.astype(np.float64)).astype(jnp.bfloat16)
    return np.concatenate([high, high, low], axis=1)


def interior(
    state_ref, adjoint_ref, gradient_ref, cell_ref, out_ref,
    held_refs, o_ref, held_cell, done_ref, out_done, told,
):
    local, fields, axial, radial = out_ref.shape
    def fetch(i):
        return [
            pltpu.make_async_copy(far_ref.at[i], near_ref.at[i % 2], done_ref.at[i % 2, n])
            for n, (far_ref, near_ref) in enumerate(
                zip((state_ref, adjoint_ref, gradient_ref), held_refs)
            )
        ]

    for copy in fetch(0):
        copy.start()
    kinds = pltpu.make_async_copy(cell_ref, held_cell, told)
    kinds.start()
    kinds.wait()
    cell = held_cell[...]
    fluid = (cell != 1).astype(jnp.float32)
    feed = (cell == 0).astype(jnp.float32) + 3.0 * (cell == 2).astype(jnp.float32)
    relax = wall_relax * (cell == 1).astype(jnp.float32)
    row = lax.broadcasted_iota(jnp.int32, (axial, radial), 0)
    lane = lax.broadcasted_iota(jnp.int32, (axial, radial), 1)
    for i in range(local):
        for copy in fetch(i):
            copy.wait()
        if i + 1 < local:
            for copy in fetch(i + 1):
                copy.start()
        held_state, held_adjoint, held_gradient = (ref.at[i % 2] for ref in held_refs)
        axial_diff, radial_diff, source, spread = [], [], [], []
        for f in range(fields):
            adjoint = held_adjoint[f]
            weighted = fluid * adjoint
            before = jnp.where(row == 0, 0.0, pltpu.roll(weighted, 1, 0))
            after = jnp.where(row == axial - 1, 0.0, pltpu.roll(weighted, axial - 1, 0))
            inward = jnp.where(lane == 0, 0.0, pltpu.roll(weighted, 1, 1))
            outward = jnp.where(lane == radial - 1, 0.0, pltpu.roll(weighted, radial - 1, 1))
            axial_diff.append(0.5 * (after - before))
            radial_diff.append(0.5 * (outward - inward))
            source.append(feed * adjoint)
            spread.append(
                dissipation * ((after + before) + (outward + inward))
                - (4.0 * dissipation) * weighted
                - relax * adjoint
                - held_gradient[f]
            )
        ion = jnp.exp(held_state[0])
        u = held_state[1]
        v = held_state[2]
        neutral = jnp.exp(held_state[3])
        temper = held_state[4]
        p, q, m = axial_diff, radial_diff, source
        ionize = ionize_rate * neutral * (m[0] - m[3])
        if i > 0:
            out.wait()
        o_ref[0] = spread[0] + ion * (u * p[0] + v * q[0])
        o_ref[1] = (
            spread[1]
            + (ion * p[0] + u * p[1] + v * (p[2] + q[1]) + temper * p[4])
            + (field_push * m[4] - collide_rate * m[1])
        )
        o_ref[2] = (
            spread[2]
            + (ion * q[0] + u * (p[2] + q[1]) + v * q[2] + 0.5 * neutral * q[3] + temper * q[4])
            - collide_rate * m[2]
        )
        o_ref[3] = spread[3] + neutral * (p[3] + 0.5 * v * q[3]) + ionize * temper
        o_ref[4] = (
            spread[4]
            + (p[1] + q[2] + u * p[4] + v * q[4])
            + (ionize + field_push * m[1] - (2.0 * energy_loss) * temper * m[4])
        )
        out = pltpu.make_async_copy(o_ref, out_ref.at[i], out_done)
        out.start()
    out.wait()


def pack_kernel(
    across, me_ref, x_ref, kind_ref, state_ref, adjoint_ref, gradient_ref, cell_ref,
    o_ref, edge_ref, rest_ref,
    held_ref, kinds_ref, done_ref, told_ref, *work,
):
    groups, chunk, size, _ = held_ref.shape

    copies = [
        pltpu.make_async_copy(x_ref.at[:, pl.ds(g * size, size), :], held_ref.at[g], done_ref.at[g])
        for g in range(groups)
    ]
    tell = pltpu.make_async_copy(kind_ref, kinds_ref, told_ref)
    for copy in copies:
        copy.start()
    tell.start()
    @pl.when(me_ref[0] % 2 == 0)
    def _():
        interior(
            state_ref, adjoint_ref, gradient_ref, cell_ref, rest_ref, work[:3], *work[3:]
        )

    for g in range(groups):
        copies[g].wait()
        rows = held_ref.at[g].reshape(chunk * size, LANES)
        for d in range(size):
            o_ref[pl.ds((g * size + d) * chunk, chunk), :] = rows[pl.ds(d, chunk, stride=size), :]
    tell.wait()
    for side, (first, row) in enumerate(((0, 0), (groups - across, size - 1))):
        for c in range(across):
            fluid = (kinds_ref[first + c, row : row + 1, :] != 1).astype(jnp.float32)
            place = ((first + c) * size + row) * chunk
            edge_ref[pl.ds((side * across + c) * chunk, chunk), :] = (
                fluid * o_ref[pl.ds(place, chunk), :]
            )


def interior_kernel(
    me_ref, early_ref, edge_ref, state_ref, adjoint_ref, gradient_ref, cell_ref,
    rest_ref, edges_ref, *work,
):
    del early_ref, edge_ref, edges_ref

    @pl.when(me_ref[0] % 2 == 1)
    def _():
        interior(
            state_ref, adjoint_ref, gradient_ref, cell_ref, rest_ref, work[:3], *work[3:]
        )


def border_kernel(before_ref, after_ref, state_ref, o_ref):
    local, fields, axial, radial = state_ref.shape
    across, chunk = radial // LANES, local * fields
    sides = ((0, -0.5, before_ref), (axial - 1, 0.5, after_ref))
    for mine, (row, sign, edge_ref) in enumerate(sides):
        for c in range(across):
            lanes = pl.ds(c * LANES, LANES)
            edges = [
                edge_ref[pl.ds(c * chunk + f, local, stride=fields), :] for f in range(fields)
            ]
            ion, u, v, neutral, temper = [state_ref[:, f, row, lanes] for f in range(fields)]
            ion, neutral = jnp.exp(ion), jnp.exp(neutral)
            p = [sign * e for e in edges]
            added = (
                ion * u * p[0],
                ion * p[0] + u * p[1] + v * p[2] + temper * p[4],
                u * p[2],
                neutral * p[3],
                p[1] + u * p[4],
            )
            for f in range(fields):
                total = dissipation * edges[f] + added[f]
                for i in range(local):
                    o_ref[mine, i * fields + f, c : c + 1, :] = total[i : i + 1, :]


def product_kernel(fields, total, d_ref, x_ref, o_ref):
    columns = jnp.concatenate(
        [x_ref[pl.ds(f, total, stride=fields), :] for f in range(fields)], axis=1
    )
    high = columns.astype(jnp.bfloat16)
    low = (columns - high.astype(jnp.float32)).astype(jnp.bfloat16)
    stacked = jnp.concatenate([high, low, high], axis=0)
    result = jnp.dot(d_ref[...], stacked, preferred_element_type=jnp.float32)
    for f in range(fields):
        o_ref[pl.ds(f, total, stride=fields), :] = result[:, f * LANES : (f + 1) * LANES]


def combine_kernel(chunk, t_ref, s_ref, b_ref, o_ref, held_ref, done_ref):
    groups, size, _ = held_ref.shape
    parts = groups * size // chunk
    copies = []
    for g in range(groups):
        for q in range(size // parts):
            tile = g * (size // parts) + q
            held_ref[g, pl.ds(q * parts, parts), :] = (
                t_ref[pl.ds(tile, parts, stride=chunk), :] + s_ref[pl.ds(tile * parts, parts), :]
            )
            across = b_ref.shape[2]
            for side, at in ((0, 0), (1, parts - across * SUB + SUB - 1)):
                held_ref[g, pl.ds(q * parts + at, across, stride=SUB), :] += b_ref[side, tile]
        copies.append(
            pltpu.make_async_copy(
                held_ref.at[g], o_ref.at[pl.ds(g * size, size), :], done_ref.at[g]
            )
        )
        copies[g].start()
    for copy in copies:
        copy.wait()


def to_tiles(x):
    local, fields, axial, radial = x.shape
    x = x.reshape(local, fields, axial // SUB, SUB, radial // LANES, LANES)
    return x.transpose(0, 1, 2, 4, 3, 5).reshape(-1, LANES)


def from_tiles(x, shape):
    local, fields, axial, radial = shape
    x = x.reshape(local, fields, axial // SUB, radial // LANES, SUB, LANES)
    return x.transpose(0, 1, 2, 4, 3, 5).reshape(shape)


def per_device(base_state, adjoint, gradient, cell_types):
    shape = adjoint.shape
    local, fields, _, radial = shape
    parts = lax.axis_size("inst")
    total = local * parts
    chunk = local * fields
    rows = adjoint.size // LANES
    far = pl.BlockSpec(memory_space=pl.ANY)
    near = pl.BlockSpec(memory_space=pltpu.VMEM)
    scalars = pl.BlockSpec(memory_space=pltpu.SMEM)
    resident = "resident"

    def run(kernel, name, outs, ins, *operands, scratch=(), flops=0, aliases=None):
        moved = sum(x.size for x in operands) + sum(o.size for o, _ in outs)
        operands = [
            pltpu.with_memory_space_constraint(x, pltpu.VMEM) if m is resident else x
            for x, m in zip(operands, ins)
        ]
        shapes = [
            pltpu.VMEM(o.shape, jnp.float32) if m is resident else o for o, m in outs
        ]
        specs = [far if m is far else near for _, m in outs]
        return pl.pallas_call(
            kernel,
            out_shape=shapes if len(shapes) > 1 else shapes[0],
            in_specs=[near if m is resident else m for m in ins],
            out_specs=specs if len(specs) > 1 else specs[0],
            scratch_shapes=list(scratch),
            input_output_aliases=aliases or {},
            name=name,
            cost_estimate=pl.CostEstimate(
                flops=flops, bytes_accessed=4 * moved, transcendentals=0
            ),
        )(*operands)

    def exchange(x):
        x = x.reshape(parts, fields, local, LANES)
        return lax.all_to_all(x, "inst", 0, 0, axis_index_groups=[order]).reshape(rows, LANES)

    first_part = FIRST_PART % parts
    order = [(first_part + p) % parts for p in range(parts)]
    flat = jax.ShapeDtypeStruct((rows, LANES), jnp.float32)
    groups = parts // SUB
    across = radial // LANES
    kinds = cell_types.reshape(-1, SUB, across, LANES).transpose(0, 2, 1, 3)
    edge = jax.ShapeDtypeStruct((2 * across * chunk, LANES), jnp.float32)
    me = lax.axis_index("space").astype(jnp.int32).reshape(1)
    whole = jax.ShapeDtypeStruct(shape, jnp.float32)
    work = [
        *[pltpu.VMEM((2, *shape[1:]), jnp.float32)] * 3,
        pltpu.VMEM(shape[1:], jnp.float32),
        pltpu.VMEM(shape[2:], jnp.int32),
        pltpu.SemaphoreType.DMA((2, 3)),
        pltpu.SemaphoreType.DMA,
        pltpu.SemaphoreType.DMA,
    ]
    packed, edges, early = run(
        lambda *r: pack_kernel(across, *r),
        "pack",
        [(flat, resident), (edge, resident), (whole, far)],
        [scalars] + [far] * 6,
        me,
        to_tiles(adjoint).reshape(chunk, parts, LANES),
        kinds.reshape(groups, SUB, LANES),
        base_state,
        adjoint,
        gradient,
        cell_types,
        scratch=[
            pltpu.VMEM((groups, chunk, SUB, LANES), jnp.float32),
            pltpu.VMEM((groups, SUB, LANES), jnp.int32),
            pltpu.SemaphoreType.DMA((groups,)),
            pltpu.SemaphoreType.DMA,
            *work,
        ],
    )
    columns = exchange(packed)
    product = run(
        lambda *r: product_kernel(fields, total, *r),
        "time_product",
        [(flat, resident)],
        [resident, resident],
        jnp.asarray(derivative_matrix(total)),
        columns,
        flops=6 * total * total * fields * LANES,
    )
    time_part = exchange(product)

    inner, edges = run(
        interior_kernel,
        "interior",
        [(whole, far), (edge, resident)],
        [scalars, far, resident, far, far, far, far],
        me,
        early,
        edges,
        base_state,
        adjoint,
        gradient,
        cell_types,
        scratch=work,
        flops=60 * adjoint.size,
        aliases={1: 0, 2: 1},
    )
    count = lax.axis_size("space")
    half = across * chunk
    up = [(i, i + 1) for i in range(count - 1)]
    down = [(i + 1, i) for i in range(count - 1)]
    borders = run(
        border_kernel,
        "border",
        [(jax.ShapeDtypeStruct((2, chunk, across, LANES), jnp.float32), resident)],
        [resident] * 3,
        lax.ppermute(edges[half:], "space", up),
        lax.ppermute(edges[:half], "space", down),
        base_state,
        flops=4 * adjoint.size,
    )
    pieces = fields
    out = run(
        lambda *r: combine_kernel(chunk, *r),
        "combine",
        [(flat, far)],
        [resident, resident, resident],
        time_part,
        to_tiles(inner),
        borders,
        scratch=[
            pltpu.VMEM((pieces, rows // pieces, LANES), jnp.float32),
            pltpu.SemaphoreType.DMA((pieces,)),
        ],
    )
    return from_tiles(out, shape)


def solution(mesh):
    return jax.shard_map(
        per_device,
        mesh=mesh,
        in_specs=(
            P("inst", None, "space", None),
            P("inst", None, "space", None),
            P("inst", None, "space", None),
            P("space", None),
        ),
        out_specs=P("inst", None, "space", None),
        check_vma=False,
    )
```

```python
import jax
import jax.numpy as jnp
import numpy as np
from jax import lax
from jax.experimental import pallas as pl
from jax.experimental.pallas import tpu as pltpu
from jax.sharding import PartitionSpec as P

dissipation = 0.5
ionize_rate = 0.6
collide_rate = 0.4
energy_loss = 0.3
field_push = 0.8
wall_relax = 2.0
time_factor = 4.0

LANES = 128
SUB = 8
FIRST_PART = 47


def derivative_matrix(total):
    gap = np.arange(total)[:, None] - np.arange(total)[None, :]
    off = gap != 0
    angle = np.where(off, np.pi * gap / total, 1.0)
    entry = np.where(off, 0.5 * np.where(gap % 2 == 0, 1.0, -1.0) / np.tan(angle), 0.0)
    entry = -(time_factor / total) * entry
    high = entry.astype(jnp.bfloat16)
    low = (entry - high.astype(np.float64)).astype(jnp.bfloat16)
    return np.concatenate([high, high, low], axis=1)


def interior(
    state_ref, adjoint_ref, gradient_ref, cell_ref, out_ref,
    held_refs, o_ref, held_cell, done_ref, out_done, told,
):
    local, fields, axial, radial = out_ref.shape
    def fetch(i):
        return [
            pltpu.make_async_copy(far_ref.at[i], near_ref.at[i % 2], done_ref.at[i % 2, n])
            for n, (far_ref, near_ref) in enumerate(
                zip((state_ref, adjoint_ref, gradient_ref), held_refs)
            )
        ]

    for copy in fetch(0):
        copy.start()
    kinds = pltpu.make_async_copy(cell_ref, held_cell, told)
    kinds.start()
    kinds.wait()
    cell = held_cell[...]
    fluid = (cell != 1).astype(jnp.float32)
    feed = (cell == 0).astype(jnp.float32) + 3.0 * (cell == 2).astype(jnp.float32)
    relax = wall_relax * (cell == 1).astype(jnp.float32)
    row = lax.broadcasted_iota(jnp.int32, (axial, radial), 0)
    lane = lax.broadcasted_iota(jnp.int32, (axial, radial), 1)
    for i in range(local):
        for copy in fetch(i):
            copy.wait()
        held_state, held_adjoint, held_gradient = (ref.at[i % 2] for ref in held_refs)
        axial_diff, radial_diff, source, spread = [], [], [], []
        for f in range(fields):
            adjoint = held_adjoint[f]
            weighted = fluid * adjoint
            before = jnp.where(row == 0, 0.0, pltpu.roll(weighted, 1, 0))
            after = jnp.where(row == axial - 1, 0.0, pltpu.roll(weighted, axial - 1, 0))
            inward = jnp.where(lane == 0, 0.0, pltpu.roll(weighted, 1, 1))
            outward = jnp.where(lane == radial - 1, 0.0, pltpu.roll(weighted, radial - 1, 1))
            axial_diff.append(0.5 * (after - before))
            radial_diff.append(0.5 * (outward - inward))
            source.append(feed * adjoint)
            spread.append(
                dissipation * ((after + before) + (outward + inward))
                - (4.0 * dissipation) * weighted
                - relax * adjoint
                - held_gradient[f]
            )
        ion = jnp.exp(held_state[0])
        u = held_state[1]
        v = held_state[2]
        neutral = jnp.exp(held_state[3])
        temper = held_state[4]
        p, q, m = axial_diff, radial_diff, source
        ionize = ionize_rate * neutral * (m[0] - m[3])
        if i > 0:
            out.wait()
        o_ref[0] = spread[0] + ion * (u * p[0] + v * q[0])
        o_ref[1] = (
            spread[1]
            + (ion * p[0] + u * p[1] + v * (p[2] + q[1]) + temper * p[4])
            + (field_push * m[4] - collide_rate * m[1])
        )
        o_ref[2] = (
            spread[2]
            + (ion * q[0] + u * (p[2] + q[1]) + v * q[2] + 0.5 * neutral * q[3] + temper * q[4])
            - collide_rate * m[2]
        )
        o_ref[3] = spread[3] + neutral * (p[3] + 0.5 * v * q[3]) + ionize * temper
        o_ref[4] = (
            spread[4]
            + (p[1] + q[2] + u * p[4] + v * q[4])
            + (ionize + field_push * m[1] - (2.0 * energy_loss) * temper * m[4])
        )
        out = pltpu.make_async_copy(o_ref, out_ref.at[i], out_done)
        out.start()
        if i + 1 < local:
            for copy in fetch(i + 1):
                copy.start()
    out.wait()


def pack_kernel(
    across, me_ref, x_ref, kind_ref, state_ref, adjoint_ref, gradient_ref, cell_ref,
    o_ref, edge_ref, rest_ref,
    held_ref, kinds_ref, done_ref, told_ref, *work,
):
    groups, chunk, size, _ = held_ref.shape

    copies = [
        pltpu.make_async_copy(x_ref.at[:, pl.ds(g * size, size), :], held_ref.at[g], done_ref.at[g])
        for g in range(groups)
    ]
    tell = pltpu.make_async_copy(kind_ref, kinds_ref, told_ref)
    for copy in copies:
        copy.start()
    tell.start()
    @pl.when(me_ref[0] % 2 == 0)
    def _():
        interior(
            state_ref, adjoint_ref, gradient_ref, cell_ref, rest_ref, work[:3], *work[3:]
        )

    for g in range(groups):
        copies[g].wait()
        rows = held_ref.at[g].reshape(chunk * size, LANES)
        for d in range(size):
            o_ref[pl.ds((g * size + d) * chunk, chunk), :] = rows[pl.ds(d, chunk, stride=size), :]
    tell.wait()
    for side, (first, row) in enumerate(((0, 0), (groups - across, size - 1))):
        for c in range(across):
            fluid = (kinds_ref[first + c, row : row + 1, :] != 1).astype(jnp.float32)
            place = ((first + c) * size + row) * chunk
            edge_ref[pl.ds((side * across + c) * chunk, chunk), :] = (
                fluid * o_ref[pl.ds(place, chunk), :]
            )


def interior_kernel(
    me_ref, early_ref, edge_ref, state_ref, adjoint_ref, gradient_ref, cell_ref,
    rest_ref, edges_ref, *work,
):
    del early_ref, edge_ref, edges_ref

    @pl.when(me_ref[0] % 2 == 1)
    def _():
        interior(
            state_ref, adjoint_ref, gradient_ref, cell_ref, rest_ref, work[:3], *work[3:]
        )


def border_kernel(before_ref, after_ref, state_ref, o_ref):
    local, fields, axial, radial = state_ref.shape
    across, chunk = radial // LANES, local * fields
    sides = ((0, -0.5, before_ref), (axial - 1, 0.5, after_ref))
    for mine, (row, sign, edge_ref) in enumerate(sides):
        for c in range(across):
            lanes = pl.ds(c * LANES, LANES)
            edges = [
                edge_ref[pl.ds(c * chunk + f, local, stride=fields), :] for f in range(fields)
            ]
            ion, u, v, neutral, temper = [state_ref[:, f, row, lanes] for f in range(fields)]
            ion, neutral = jnp.exp(ion), jnp.exp(neutral)
            p = [sign * e for e in edges]
            added = (
                ion * u * p[0],
                ion * p[0] + u * p[1] + v * p[2] + temper * p[4],
                u * p[2],
                neutral * p[3],
                p[1] + u * p[4],
            )
            for f in range(fields):
                total = dissipation * edges[f] + added[f]
                for i in range(local):
                    o_ref[mine, i * fields + f, c : c + 1, :] = total[i : i + 1, :]


def product_kernel(fields, total, d_ref, x_ref, o_ref):
    columns = jnp.concatenate(
        [x_ref[pl.ds(f, total, stride=fields), :] for f in range(fields)], axis=1
    )
    high = columns.astype(jnp.bfloat16)
    low = (columns - high.astype(jnp.float32)).astype(jnp.bfloat16)
    stacked = jnp.concatenate([high, low, high], axis=0)
    result = jnp.dot(d_ref[...], stacked, preferred_element_type=jnp.float32)
    for f in range(fields):
        o_ref[pl.ds(f, total, stride=fields), :] = result[:, f * LANES : (f + 1) * LANES]


def combine_kernel(chunk, t_ref, s_ref, b_ref, o_ref, held_ref, done_ref):
    groups, size, _ = held_ref.shape
    parts = groups * size // chunk
    copies = []
    for g in range(groups):
        for q in range(size // parts):
            tile = g * (size // parts) + q
            held_ref[g, pl.ds(q * parts, parts), :] = (
                t_ref[pl.ds(tile, parts, stride=chunk), :] + s_ref[pl.ds(tile * parts, parts), :]
            )
            across = b_ref.shape[2]
            for side, at in ((0, 0), (1, parts - across * SUB + SUB - 1)):
                held_ref[g, pl.ds(q * parts + at, across, stride=SUB), :] += b_ref[side, tile]
        copies.append(
            pltpu.make_async_copy(
                held_ref.at[g], o_ref.at[pl.ds(g * size, size), :], done_ref.at[g]
            )
        )
        copies[g].start()
    for copy in copies:
        copy.wait()


def to_tiles(x):
    local, fields, axial, radial = x.shape
    x = x.reshape(local, fields, axial // SUB, SUB, radial // LANES, LANES)
    return x.transpose(0, 1, 2, 4, 3, 5).reshape(-1, LANES)


def from_tiles(x, shape):
    local, fields, axial, radial = shape
    x = x.reshape(local, fields, axial // SUB, radial // LANES, SUB, LANES)
    return x.transpose(0, 1, 2, 4, 3, 5).reshape(shape)


def per_device(base_state, adjoint, gradient, cell_types):
    shape = adjoint.shape
    local, fields, _, radial = shape
    parts = lax.axis_size("inst")
    total = local * parts
    chunk = local * fields
    rows = adjoint.size // LANES
    far = pl.BlockSpec(memory_space=pl.ANY)
    near = pl.BlockSpec(memory_space=pltpu.VMEM)
    scalars = pl.BlockSpec(memory_space=pltpu.SMEM)
    resident = "resident"

    def run(kernel, name, outs, ins, *operands, scratch=(), flops=0, aliases=None):
        moved = sum(x.size for x in operands) + sum(o.size for o, _ in outs)
        operands = [
            pltpu.with_memory_space_constraint(x, pltpu.VMEM) if m is resident else x
            for x, m in zip(operands, ins)
        ]
        shapes = [
            pltpu.VMEM(o.shape, jnp.float32) if m is resident else o for o, m in outs
        ]
        specs = [far if m is far else near for _, m in outs]
        return pl.pallas_call(
            kernel,
            out_shape=shapes if len(shapes) > 1 else shapes[0],
            in_specs=[near if m is resident else m for m in ins],
            out_specs=specs if len(specs) > 1 else specs[0],
            scratch_shapes=list(scratch),
            input_output_aliases=aliases or {},
            name=name,
            cost_estimate=pl.CostEstimate(
                flops=flops, bytes_accessed=4 * moved, transcendentals=0
            ),
        )(*operands)

    def exchange(x):
        x = x.reshape(parts, fields, local, LANES)
        return lax.all_to_all(x, "inst", 0, 0, axis_index_groups=[order]).reshape(rows, LANES)

    first_part = FIRST_PART % parts
    order = [(first_part + p) % parts for p in range(parts)]
    flat = jax.ShapeDtypeStruct((rows, LANES), jnp.float32)
    groups = parts // SUB
    across = radial // LANES
    kinds = cell_types.reshape(-1, SUB, across, LANES).transpose(0, 2, 1, 3)
    edge = jax.ShapeDtypeStruct((2 * across * chunk, LANES), jnp.float32)
    me = lax.axis_index("space").astype(jnp.int32).reshape(1)
    whole = jax.ShapeDtypeStruct(shape, jnp.float32)
    work = [
        *[pltpu.VMEM((2, *shape[1:]), jnp.float32)] * 3,
        pltpu.VMEM(shape[1:], jnp.float32),
        pltpu.VMEM(shape[2:], jnp.int32),
        pltpu.SemaphoreType.DMA((2, 3)),
        pltpu.SemaphoreType.DMA,
        pltpu.SemaphoreType.DMA,
    ]
    packed, edges, early = run(
        lambda *r: pack_kernel(across, *r),
        "pack",
        [(flat, resident), (edge, resident), (whole, far)],
        [scalars] + [far] * 6,
        me,
        to_tiles(adjoint).reshape(chunk, parts, LANES),
        kinds.reshape(groups, SUB, LANES),
        base_state,
        adjoint,
        gradient,
        cell_types,
        scratch=[
            pltpu.VMEM((groups, chunk, SUB, LANES), jnp.float32),
            pltpu.VMEM((groups, SUB, LANES), jnp.int32),
            pltpu.SemaphoreType.DMA((groups,)),
            pltpu.SemaphoreType.DMA,
            *work,
        ],
    )
    columns = exchange(packed)
    product = run(
        lambda *r: product_kernel(fields, total, *r),
        "time_product",
        [(flat, resident)],
        [resident, resident],
        jnp.asarray(derivative_matrix(total)),
        columns,
        flops=6 * total * total * fields * LANES,
    )
    time_part = exchange(product)

    inner, edges = run(
        interior_kernel,
        "interior",
        [(whole, far), (edge, resident)],
        [scalars, far, resident, far, far, far, far],
        me,
        early,
        edges,
        base_state,
        adjoint,
        gradient,
        cell_types,
        scratch=work,
        flops=60 * adjoint.size,
        aliases={1: 0, 2: 1},
    )
    count = lax.axis_size("space")
    half = across * chunk
    up = [(i, i + 1) for i in range(count - 1)]
    down = [(i + 1, i) for i in range(count - 1)]
    borders = run(
        border_kernel,
        "border",
        [(jax.ShapeDtypeStruct((2, chunk, across, LANES), jnp.float32), resident)],
        [resident] * 3,
        lax.ppermute(edges[half:], "space", up),
        lax.ppermute(edges[:half], "space", down),
        base_state,
        flops=4 * adjoint.size,
    )
    pieces = fields
    out = run(
        lambda *r: combine_kernel(chunk, *r),
        "combine",
        [(flat, far)],
        [resident, resident, resident],
        time_part,
        to_tiles(inner),
        borders,
        scratch=[
            pltpu.VMEM((pieces, rows // pieces, LANES), jnp.float32),
            pltpu.SemaphoreType.DMA((pieces,)),
        ],
    )
    return from_tiles(out, shape)


def solution(mesh):
    return jax.shard_map(
        per_device,
        mesh=mesh,
        in_specs=(
            P("inst", None, "space", None),
            P("inst", None, "space", None),
            P("inst", None, "space", None),
            P("space", None),
        ),
        out_specs=P("inst", None, "space", None),
        check_vma=False,
    )
```
